512 devices in a mesh: dp: 64 (over z, x), tensor: 8 (over y, core).
Axes of the slice: x: 4, y: 4, z: 16, core: 2. Of those that a mesh axis runs over, the one named last changes fastest.
Arguments:
- gradient: float32 [64, 512, 4096], P('dp', 'tensor'), may hold values from -90 to 90
- error_buffer: float32 [64, 512, 4096], P('dp', 'tensor'), may hold values from -6 to 6
- right_factor: float32 [4096, 32], replicated, may hold values from -6 to 6
Outputs:
- averaged: float32 [512, 4096], P('tensor')
- new_error: float32 [64, 512, 4096], P('dp', 'tensor')
The draws below stay inside these ranges and needn't reach their ends.
All inputs are finite; a program needn't handle non-finite values.
Results may differ from the reference program's by a relative error of at most 0.0003.
Values sent between devices are 32-bit elements; how exact they have to be, the bound alone decides.
No kernel may reach another device: no remote copies, remote signals or barrier semaphores. Data moves between devices by JAX's collectives and lax.ppermute only.
A program may use at most 64 MiB of HBM per device.

```python
import math
import jax
import jax.numpy as jnp
from jax import lax

N = 4096
RANK = 32
ROWS = 512
REPLICAS = 64


def draw_gradient(key, part):
    key = jax.random.fold_in(key, 11)
    k_base, k_rows, k_cols = jax.random.split(key, 3)
    steps = jnp.arange(REPLICAS, dtype=jnp.float32) / max(REPLICAS - 1, 1)
    replica_scale = 1.0 + 2.0 * steps
    row_scale = jnp.exp(jax.random.uniform(k_rows, (ROWS,), jnp.float32, 0.0, math.log(10.0)))
    col_scale = jnp.exp(jax.random.uniform(k_cols, (N,), jnp.float32, 0.0, math.log(10.0)))
    base = jnp.clip(jax.random.normal(k_base, (REPLICAS, ROWS, N), jnp.float32), -6.0, 6.0)
    values = 0.05 * base * replica_scale[:, None, None] * row_scale[None, :, None] * col_scale[None, None, :]
    return values.astype(jnp.float32)


def block_levels(own_key, extent, cuts, least, largest):
    loudness, own = 1.0, jax.random.fold_in(own_key, 6)
    for axis_at, parts in cuts:
        steps = jnp.exp(jax.random.uniform(jax.random.fold_in(own, axis_at), (parts,), jnp.float32, least / len(cuts), largest / len(cuts)))
        loudness = loudness * jnp.repeat(steps, extent[axis_at] // parts).reshape([-1 if axis == axis_at else 1 for axis in range(len(extent))])
    return loudness


def centred(stream_key, extent, width, reach, shards=(), kind=jnp.bfloat16):
    drawn = width * jax.random.normal(stream_key, extent, jnp.float32)
    if shards:
        drawn = drawn * block_levels(stream_key, extent, shards, -0.22, 0.18)
    return jnp.clip(drawn, -reach, reach).astype(kind)


def setup_inputs(seed: int = 0) -> dict:
    key_list = jax.random.split(jax.random.key(seed), 4)
    return {
        "gradient": draw_gradient(jax.random.fold_in(key_list[3], 71), 0),
        "error_buffer": centred(key_list[1], (REPLICAS, ROWS, N), 0.5, 6.0, ((0, 64), (1, 8)), jnp.float32),
        "right_factor": centred(key_list[2], (N, RANK), 1.0, 6.0, (), jnp.float32),
    }


def reference(gradient, error_buffer, right_factor):
    highest = lax.Precision.HIGHEST
    corrected = gradient + error_buffer
    left_sum = jnp.einsum('rmn,nk->mk', corrected, right_factor, precision=highest)
    gram = jnp.dot(left_sum.T, left_sum, precision=highest)
    lower = jnp.linalg.cholesky(gram)
    basis = lax.linalg.triangular_solve(lower, left_sum, left_side=False, lower=True, transpose_a=True)
    new_right = jnp.einsum('rmn,mk->nk', corrected, basis, precision=highest) / REPLICAS
    averaged = jnp.dot(basis, new_right.T, precision=highest)
    new_error = corrected - averaged[None]
    return (averaged, new_error)
```

```python
import jax
import jax.numpy as jnp
from jax import lax
from jax.sharding import Mesh, PartitionSpec as P

AXES = ("z", "x", "y", "core")


def copies(block, axis):
    count = lax.axis_size(axis)
    return lax.all_to_all(jnp.broadcast_to(block[None], (count,) + block.shape), axis, 0, 0)


def pack(matrix):
    rows = matrix.shape[0]
    return matrix.reshape(4, rows // 4, 32).transpose(1, 0, 2).reshape(rows // 4, 128)


def unpack(dense):
    rows = dense.shape[0]
    return dense.reshape(rows, 4, 32).transpose(1, 0, 2).reshape(rows * 4, 32)


def shards(gradient, error_buffer, right_factor):
    highest = lax.Precision.HIGHEST
    rank = right_factor.shape[1]
    width = right_factor.shape[0]
    corrected = gradient[0] + error_buffer[0]
    local_left = pack(jnp.dot(corrected, right_factor, precision=highest))
    left_sum = unpack(copies(copies(local_left, "x").sum(0), "z").sum(0))
    plane = ("x", "y", "core")
    peers = lax.axis_size(plane)
    share = width // peers
    part = lax.dot_general(left_sum, corrected, (((0,), (0,)), ((), ())), precision=highest)
    part = part.reshape(rank, peers, share).transpose(1, 0, 2)
    gram = pack(lax.dot_general(left_sum, left_sum, (((0,), (0,)), ((), ())), precision=highest))
    sent = jnp.concatenate([part, jnp.broadcast_to(gram[None], (peers,) + gram.shape)], axis=1)
    got = lax.all_to_all(sent, plane, 0, 0).sum(0)
    gram = unpack(got[rank:]) / lax.axis_size("x")
    mine = copies(got[:rank], "z").sum(0)
    whole = lax.all_gather(copies(mine, ("x", "y")), "core")
    whole = whole.transpose(2, 1, 0, 3).reshape(rank, width)
    lower = jnp.linalg.cholesky(gram)
    basis = lax.linalg.triangular_solve(
        lower, left_sum, left_side=False, lower=True, transpose_a=True
    )
    back = lax.linalg.triangular_solve(
        lower, basis, left_side=False, lower=True, transpose_a=False
    )
    replicas = lax.axis_size("z") * lax.axis_size("x")
    averaged = jnp.dot(back, whole, precision=highest) / replicas
    new_error = (corrected - averaged)[None]
    return (averaged, new_error)


def solution(mesh):
    fine = Mesh(mesh.devices.reshape(16, 4, 4, 2), AXES)
    in_specs = (P(("z", "x"), ("y", "core"), None), P(("z", "x"), ("y", "core"), None), P())
    out_specs = (P(("y", "core"), None), P(("z", "x"), ("y", "core"), None))
    return jax.shard_map(shards, mesh=fine, in_specs=in_specs, out_specs=out_specs, check_vma=False)
```

```python
import jax
import jax.numpy as jnp
from jax import lax
from jax.sharding import Mesh, PartitionSpec as P

AXES = ("far", "near", "x", "y", "core")
DP = ("far", "near", "x")
TENSOR = ("y", "core")
HIGHEST = lax.Precision.HIGHEST


def copies(block, axis):
    count = lax.axis_size(axis)
    return lax.all_to_all(jnp.broadcast_to(block[None], (count,) + block.shape), axis, 0, 0)


def pack(matrix):
    rows = matrix.shape[0]
    return matrix.reshape(4, rows // 4, 32).transpose(1, 0, 2).reshape(rows // 4, 128)


def unpack(dense):
    rows = dense.shape[0]
    return dense.reshape(rows, 4, 32).transpose(1, 0, 2).reshape(rows * 4, 32)


def shards(gradient, error_buffer, right_factor):
    width, rank = right_factor.shape
    columns, near, tensor = lax.axis_size("x"), lax.axis_size("near"), lax.axis_size(TENSOR)
    span = width // columns
    share = span // tensor
    half = rank // near
    corrected = gradient[0] + error_buffer[0]
    local_left = pack(jnp.dot(corrected, right_factor, precision=HIGHEST))
    left_sum = unpack(copies(copies(local_left, "x").sum(0), ("far", "near")).sum(0))

    here = lax.axis_index("x")

    def block(at):
        return lax.dynamic_slice_in_dim(corrected, lax.rem(here + at, columns) * span, span, axis=1)

    moved = block(0)
    for step in range(1, columns):
        ring = [(i, (i + step) % columns) for i in range(columns)]
        moved = moved + lax.ppermute(block(step), "x", ring)

    part = lax.dot_general(left_sum, moved, (((0,), (0,)), ((), ())), precision=HIGHEST)
    part = part.reshape(near, half, tensor, share).transpose(0, 2, 1, 3).reshape(near * tensor, half, share)
    gram = pack(lax.dot_general(left_sum, left_sum, (((0,), (0,)), ((), ())), precision=HIGHEST))
    sent = jnp.concatenate([part, jnp.broadcast_to(gram[None], (near * tensor,) + gram.shape)], axis=1)
    got = lax.all_to_all(sent, ("near",) + TENSOR, 0, 0).sum(0)
    gram = unpack(got[half:]) / near
    mine = copies(got[:half], "far").sum(0)
    whole = lax.all_gather(copies(mine, ("near", "x", "y")), "core")
    whole = whole.reshape(2, near, columns, tensor // 2, half, share).transpose(1, 4, 2, 3, 0, 5)
    whole = whole.reshape(rank, width)

    lower = jnp.linalg.cholesky(gram)
    basis = lax.linalg.triangular_solve(
        lower, left_sum, left_side=False, lower=True, transpose_a=True
    )
    back = lax.linalg.triangular_solve(
        lower, basis, left_side=False, lower=True, transpose_a=False
    )
    averaged = jnp.dot(back, whole, precision=HIGHEST) / lax.axis_size(DP)
    new_error = (corrected - averaged)[None]
    return (averaged, new_error)


def solution(mesh):
    fine = Mesh(mesh.devices.reshape(8, 2, 4, 4, 2), AXES)
    in_specs = (P(DP, TENSOR, None), P(DP, TENSOR, None), P())
    out_specs = (P(TENSOR, None), P(DP, TENSOR, None))
    return jax.shard_map(shards, mesh=fine, in_specs=in_specs, out_specs=out_specs, check_vma=False)
```

```python
import jax
import jax.numpy as jnp
from jax import lax
from jax.experimental import pallas as pl
from jax.experimental.pallas import tpu as pltpu
from jax.sharding import Mesh, PartitionSpec as P

AXES = ("far", "near", "x", "y", "core")
DP = ("far", "near", "x")
TENSOR = ("y", "core")
CLOSE = ("near", "x")
HIGHEST = lax.Precision.HIGHEST
LANES = 128
VMEM_LIMIT = 16 * 2**20


def copies(block, axis):
    count = lax.axis_size(axis)
    return lax.all_to_all(jnp.broadcast_to(block[None], (count,) + block.shape), axis, 0, 0)


def pack(matrix):
    rows = matrix.shape[0]
    return matrix.reshape(4, rows // 4, 32).transpose(1, 0, 2).reshape(rows // 4, 128)


def unpack(dense):
    rows = dense.shape[0]
    return dense.reshape(rows, 4, 32).transpose(1, 0, 2).reshape(rows * 4, 32)


def beside(blocks, small):
    return jnp.concatenate([blocks, jnp.broadcast_to(small[None], blocks.shape[:1] + small.shape)], axis=1)


def first_kernel(gradient_ref, error_ref, right_ref, sent_ref, left_ref):
    step = pl.program_id(0)
    rows, span = gradient_ref.shape[1:]
    rank = right_ref.shape[0]
    corrected = gradient_ref[0] + error_ref[0]
    for tile in range(span // LANES):
        sent_ref[step, tile * rows : (tile + 1) * rows, :] = corrected[:, tile * LANES : (tile + 1) * LANES]
    part = lax.dot_general(
        corrected, right_ref[...], (((1,), (1,)), ((), ())), precision=HIGHEST, preferred_element_type=jnp.float32
    )

    @pl.when(step == 0)
    def _():
        left_ref[...] = part

    @pl.when(step > 0)
    def _():
        left_ref[...] += part

    @pl.when(step == pl.num_programs(0) - 1)
    def _():
        groups = LANES // rank
        high = rows // groups
        dense = jnp.concatenate([left_ref[g * high : (g + 1) * high, :] for g in range(groups)], axis=1)
        for block in range(sent_ref.shape[0]):
            sent_ref[block, span // LANES * rows :, :] = dense


def first(gradient, error_buffer, right, blocks):
    rank, width = right.shape
    rows = gradient.shape[1]
    span = width // blocks
    height = rows * span // LANES + rows * rank // LANES
    return pl.pallas_call(
        first_kernel,
        grid=(blocks,),
        in_specs=[
            pl.BlockSpec((1, rows, span), lambda i: (0, 0, i)),
            pl.BlockSpec((1, rows, span), lambda i: (0, 0, i)),
            pl.BlockSpec((rank, span), lambda i: (0, i)),
        ],
        out_specs=pl.BlockSpec((blocks, height, LANES), lambda i: (0, 0, 0)),
        out_shape=jax.ShapeDtypeStruct((blocks, height, LANES), jnp.float32),
        scratch_shapes=[pltpu.VMEM((rows, rank), jnp.float32)],
        compiler_params=pltpu.CompilerParams(vmem_limit_bytes=VMEM_LIMIT),
    )(gradient, error_buffer, right)


def last_kernel(back_ref, whole_ref, sent_ref, averaged_ref, error_ref):
    rows = back_ref.shape[0]
    low = lax.broadcasted_iota(jnp.int32, whole_ref.shape[2:], 1) < LANES // 2
    for block in range(whole_ref.shape[0]):
        upper, lower = [], []
        for pair in range(whole_ref.shape[1] // 2):
            even, odd = whole_ref[block, 2 * pair], whole_ref[block, 2 * pair + 1]
            upper.append(jnp.where(low, even, pltpu.roll(odd, LANES // 2, 1)))
            lower.append(jnp.where(low, pltpu.roll(even, LANES // 2, 1), odd))
        right = jnp.concatenate([jnp.concatenate(upper, axis=1), jnp.concatenate(lower, axis=1)], axis=0)
        averaged = jnp.dot(back_ref[...], right, precision=HIGHEST, preferred_element_type=jnp.float32)
        span = averaged.shape[1]
        averaged_ref[:, block * span : (block + 1) * span] = averaged
        for tile in range(span // LANES):
            columns = slice(block * span + tile * LANES, block * span + (tile + 1) * LANES)
            error_ref[0, :, columns] = (
                sent_ref[block, tile * rows : (tile + 1) * rows, :] - averaged[:, tile * LANES : (tile + 1) * LANES]
            )


def last(back, whole, sent, steps):
    rows, rank = back.shape
    blocks, height = sent.shape[0], sent.shape[1]
    each = blocks // steps
    span = whole.shape[1] * LANES // 2
    return pl.pallas_call(
        last_kernel,
        grid=(steps,),
        in_specs=[
            pl.BlockSpec((rows, rank), lambda i: (0, 0)),
            pl.BlockSpec((each,) + whole.shape[1:], lambda i: (i, 0, 0, 0)),
            pl.BlockSpec((each, height, LANES), lambda i: (i, 0, 0)),
        ],
        out_specs=[
            pl.BlockSpec((rows, each * span), lambda i: (0, i)),
            pl.BlockSpec((1, rows, each * span), lambda i: (0, 0, i)),
        ],
        out_shape=[
            jax.ShapeDtypeStruct((rows, blocks * span), jnp.float32),
            jax.ShapeDtypeStruct((1, rows, blocks * span), jnp.float32),
        ],
        compiler_params=pltpu.CompilerParams(vmem_limit_bytes=VMEM_LIMIT),
    )(back, whole, sent)


def shards(gradient, error_buffer, right_factor):
    width, rank = right_factor.shape
    rows = gradient.shape[1]
    close, far = lax.axis_size(CLOSE), lax.axis_size("far")
    tiles = width // close // LANES

    sent = first(gradient, error_buffer, right_factor.T, close)
    got = lax.all_to_all(sent, CLOSE, 0, 0).sum(0)
    blocks = got[: tiles * rows].reshape(tiles, 2, rows // 2, 2, LANES // 2).transpose(0, 3, 2, 1, 4)
    blocks = blocks.reshape(far, rows // 2, LANES)
    got = lax.all_to_all(beside(blocks, got[tiles * rows :]), "far", 0, 0).sum(0)
    left_sum = unpack(got[rows // 2 :])
    own = jnp.concatenate([got[: rows // 2, : LANES // 2], got[: rows // 2, LANES // 2 :]], axis=0)

    part = lax.dot_general(left_sum, own, (((0,), (0,)), ((), ())), precision=HIGHEST)
    part = jnp.concatenate([part[: rank // 2], part[rank // 2 :]], axis=1)
    gram = pack(lax.dot_general(left_sum, left_sum, (((0,), (0,)), ((), ())), precision=HIGHEST))
    got = copies(jnp.concatenate([part, gram], axis=0), TENSOR).sum(0)
    gram = unpack(got[rank // 2 :])
    whole = copies(got[: rank // 2], "far")

    lower = jnp.linalg.cholesky(gram)
    basis = lax.linalg.triangular_solve(
        lower, left_sum, left_side=False, lower=True, transpose_a=True
    )
    back = lax.linalg.triangular_solve(
        lower, basis, left_side=False, lower=True, transpose_a=False
    ) / lax.axis_size(DP)
    whole, back = lax.optimization_barrier((whole, back))
    whole = copies(whole, CLOSE)
    averaged, new_error = last(back, whole, sent, 4)
    return (averaged, new_error)


def solution(mesh):
    fine = Mesh(mesh.devices.reshape(8, 2, 4, 4, 2), AXES)
    in_specs = (P(DP, TENSOR, None), P(DP, TENSOR, None), P())
    out_specs = (P(TENSOR, None), P(DP, TENSOR, None))
    return jax.shard_map(shards, mesh=fine, in_specs=in_specs, out_specs=out_specs, check_vma=False)
```

```python
import functools

import jax
import jax.numpy as jnp
from jax import lax
from jax.experimental import pallas as pl
from jax.experimental.pallas import tpu as pltpu
from jax.sharding import Mesh, PartitionSpec as P

AXES = ("far", "near", "x", "y", "core")
DP = ("far", "near", "x")
TENSOR = ("y", "core")
CLOSE = ("near", "x")
HIGHEST = lax.Precision.HIGHEST
LANES = 128
SOME_VMEM = 16 * 2**20


def copies(block, axis):
    count = lax.axis_size(axis)
    return lax.all_to_all(jnp.broadcast_to(block[None], (count,) + block.shape), axis, 0, 0)


def pack(matrix):
    rows = matrix.shape[0]
    return matrix.reshape(4, rows // 4, 32).transpose(1, 0, 2).reshape(rows // 4, 128)


def unpack(dense):
    rows = dense.shape[0]
    return dense.reshape(rows, 4, 32).transpose(1, 0, 2).reshape(rows * 4, 32)


def beside(blocks, small):
    return jnp.concatenate([blocks, jnp.broadcast_to(small[None], blocks.shape[:1] + small.shape)], axis=1)


def first_kernel(corrected_ref, right_ref, sent_ref):
    rows, width = corrected_ref.shape
    rank, count = right_ref.shape[0], sent_ref.shape[0]
    span = width // count
    tiles = span // LANES
    total = None
    for block in range(count):
        columns = slice(block * span, (block + 1) * span)
        corrected = corrected_ref[:, columns]
        for tile in range(tiles):
            sent_ref[block, tile * rows : (tile + 1) * rows, :] = corrected[:, tile * LANES : (tile + 1) * LANES]
        part = lax.dot_general(
            corrected, right_ref[:, columns], (((1,), (1,)), ((), ())), precision=HIGHEST, preferred_element_type=jnp.float32
        )
        total = part if total is None else total + part
    groups = LANES // rank
    high = rows // groups
    dense = jnp.concatenate([total[g * high : (g + 1) * high, :] for g in range(groups)], axis=1)
    for block in range(count):
        sent_ref[block, tiles * rows :, :] = dense


def first(corrected, right, blocks):
    rank, width = right.shape
    rows = corrected.shape[0]
    height = rows * (width // blocks) // LANES + rows * rank // LANES
    near = pl.BlockSpec(memory_space=pltpu.VMEM)
    return pl.pallas_call(
        first_kernel,
        in_specs=[near, near],
        out_specs=near,
        out_shape=jax.ShapeDtypeStruct((blocks, height, LANES), jnp.float32),
        compiler_params=pltpu.CompilerParams(vmem_limit_bytes=SOME_VMEM),
    )(corrected, right)


def solve_kernel(gram_ref, left_ref, back_ref, *, replicas):
    rank = left_ref.shape[1]
    small = gram_ref[0]
    for peer in range(1, gram_ref.shape[0]):
        small += gram_ref[peer]
    gram = jnp.concatenate([small[:, g * rank : (g + 1) * rank] for g in range(LANES // rank)], axis=0)
    row_of = lax.broadcasted_iota(jnp.int32, (rank, rank), 0)
    unit = row_of == lax.broadcasted_iota(jnp.int32, (rank, rank), 1)
    both = jnp.concatenate([gram, unit.astype(jnp.float32)], axis=1)
    below = lax.broadcasted_iota(jnp.int32, (rank, 1), 0)
    for k in range(rank):
        factor = jnp.where(below > k, both[:, k : k + 1], 0.0) / both[k : k + 1, k : k + 1]
        both = both - factor * both[k : k + 1, :]
    pivots = jnp.sum(jnp.where(unit, both[:, :rank], 0.0), axis=0, keepdims=True)
    inverse = both[:, rank:]
    basis = lax.dot_general(
        left_ref[...], inverse, (((1,), (1,)), ((), ())), precision=HIGHEST, preferred_element_type=jnp.float32
    )
    basis = basis / (pivots * replicas)
    back_ref[...] = jnp.dot(basis, inverse, precision=HIGHEST, preferred_element_type=jnp.float32)


def solve(gram, left_sum, replicas):
    peers, height, lanes = gram.shape
    rows, rank = left_sum.shape
    high = rank * rank // LANES
    return pl.pallas_call(
        functools.partial(solve_kernel, replicas=float(replicas)),
        grid=(1,),
        in_specs=[
            pl.BlockSpec((peers, high, lanes), lambda i: (0, height // high - 1, 0)),
            pl.BlockSpec((rows, rank), lambda i: (0, 0)),
        ],
        out_specs=pl.BlockSpec((rows, rank), lambda i: (0, 0)),
        out_shape=jax.ShapeDtypeStruct((rows, rank), jnp.float32),
        compiler_params=pltpu.CompilerParams(vmem_limit_bytes=SOME_VMEM),
        cost_estimate=pl.CostEstimate(flops=4 * rank**3, bytes_accessed=2 * rows * LANES * 4, transcendentals=rank * rank),
    )(gram, left_sum)


def last_kernel(back_ref, whole_ref, sent_ref, averaged_ref, error_ref, averaged, error, leave):
    rows = back_ref.shape[0]
    count, pairs = whole_ref.shape[0], whole_ref.shape[1] // 2
    span = pairs * LANES
    low = lax.broadcasted_iota(jnp.int32, whole_ref.shape[2:], 1) < LANES // 2
    going = []
    for block in range(count):
        upper, lower = [], []
        for pair in range(pairs):
            even, odd = whole_ref[block, 2 * pair], whole_ref[block, 2 * pair + 1]
            upper.append(jnp.where(low, even, pltpu.roll(odd, LANES // 2, 1)))
            lower.append(jnp.where(low, pltpu.roll(even, LANES // 2, 1), odd))
        right = jnp.concatenate([jnp.concatenate(upper, axis=1), jnp.concatenate(lower, axis=1)], axis=0)
        columns = pl.ds(block * span, span)
        found = jnp.dot(back_ref[...], right, precision=HIGHEST, preferred_element_type=jnp.float32)
        averaged[block] = found
        for tile in range(pairs):
            lanes = slice(tile * LANES, (tile + 1) * LANES)
            error[block, :, lanes] = sent_ref[block, tile * rows : (tile + 1) * rows, :] - found[:, lanes]
        going.append(pltpu.make_async_copy(averaged.at[block], averaged_ref.at[:, columns], leave.at[0, block]))
        going.append(pltpu.make_async_copy(error.at[block], error_ref.at[0, :, columns], leave.at[1, block]))
        going[-2].start()
        going[-1].start()
    for copy in going:
        copy.wait()


def last(back, whole, sent):
    rows = back.shape[0]
    blocks = sent.shape[0]
    span = whole.shape[1] * LANES // 2
    near, anywhere = pl.BlockSpec(memory_space=pltpu.VMEM), pl.BlockSpec(memory_space=pl.ANY)
    return pl.pallas_call(
        last_kernel,
        in_specs=[near, near, near],
        out_specs=[anywhere, anywhere],
        out_shape=[
            jax.ShapeDtypeStruct((rows, blocks * span), jnp.float32),
            jax.ShapeDtypeStruct((1, rows, blocks * span), jnp.float32),
        ],
        scratch_shapes=[
            pltpu.VMEM((blocks, rows, span), jnp.float32),
            pltpu.VMEM((blocks, rows, span), jnp.float32),
            pltpu.SemaphoreType.DMA((2, blocks)),
        ],
        compiler_params=pltpu.CompilerParams(vmem_limit_bytes=SOME_VMEM),
    )(back, whole, sent)


def shards(gradient, error_buffer, right_factor):
    width, rank = right_factor.shape
    rows = gradient.shape[1]
    close, far = lax.axis_size(CLOSE), lax.axis_size("far")
    tiles = width // close // LANES

    corrected = gradient[0] + error_buffer[0]
    sent = first(corrected, right_factor.T, close)
    got = lax.all_to_all(sent, CLOSE, 0, 0).sum(0)
    blocks = got[: tiles * rows].reshape(tiles, 2, rows // 2, 2, LANES // 2).transpose(0, 3, 2, 1, 4)
    blocks = blocks.reshape(far, rows // 2, LANES)
    got = lax.all_to_all(beside(blocks, got[tiles * rows :]), "far", 0, 0).sum(0)
    left_sum = unpack(got[rows // 2 :])
    own = jnp.concatenate([got[: rows // 2, : LANES // 2], got[: rows // 2, LANES // 2 :]], axis=0)

    part = lax.dot_general(left_sum, own, (((0,), (0,)), ((), ())), precision=HIGHEST)
    part = jnp.concatenate([part[: rank // 2], part[rank // 2 :]], axis=1)
    gram = pack(lax.dot_general(left_sum, left_sum, (((0,), (0,)), ((), ())), precision=HIGHEST))
    got = copies(jnp.concatenate([part, gram], axis=0), TENSOR)
    back = solve(got, left_sum, lax.axis_size(DP))
    whole = copies(copies(got[:, : rank // 2].sum(0), "far"), CLOSE)
    averaged, new_error = last(back, whole, sent)
    return (averaged, new_error)


def solution(mesh):
    fine = Mesh(mesh.devices.reshape(8, 2, 4, 4, 2), AXES)
    in_specs = (P(DP, TENSOR, None), P(DP, TENSOR, None), P())
    out_specs = (P(TENSOR, None), P(DP, TENSOR, None))
    return jax.shard_map(shards, mesh=fine, in_specs=in_specs, out_specs=out_specs, check_vma=False)
```

```python
import functools

import jax
import jax.numpy as jnp
from jax import lax
from jax.experimental import pallas as pl
from jax.experimental.pallas import tpu as pltpu
from jax.sharding import Mesh, PartitionSpec as P

AXES = ("far", "near", "x", "y", "core")
DP = ("far", "near", "x")
TENSOR = ("y", "core")
CLOSE = ("near", "x")
HIGHEST = lax.Precision.HIGHEST
LANES = 128
SOME_VMEM = 16 * 2**20


def copies(block, axis):
    count = lax.axis_size(axis)
    return lax.all_to_all(jnp.broadcast_to(block[None], (count,) + block.shape), axis, 0, 0)


def first_kernel(corrected_ref, right_ref, sent_ref):
    rows, width = corrected_ref.shape
    rank, count = right_ref.shape[0], sent_ref.shape[0]
    span = width // count
    tiles = span // LANES
    total = None
    for block in range(count):
        columns = slice(block * span, (block + 1) * span)
        corrected = corrected_ref[:, columns]
        for tile in range(tiles):
            sent_ref[block, tile * rows : (tile + 1) * rows, :] = corrected[:, tile * LANES : (tile + 1) * LANES]
        part = lax.dot_general(
            corrected, right_ref[:, columns], (((1,), (1,)), ((), ())), precision=HIGHEST, preferred_element_type=jnp.float32
        )
        total = part if total is None else total + part
    groups = LANES // rank
    high = rows // groups
    dense = jnp.concatenate([total[g * high : (g + 1) * high, :] for g in range(groups)], axis=1)
    for block in range(count):
        sent_ref[block, tiles * rows :, :] = dense


def first(corrected, right, blocks):
    rank, width = right.shape
    rows = corrected.shape[0]
    height = rows * (width // blocks) // LANES + rows * rank // LANES
    near = pl.BlockSpec(memory_space=pltpu.VMEM)
    return pl.pallas_call(
        first_kernel,
        in_specs=[near, near],
        out_specs=near,
        out_shape=jax.ShapeDtypeStruct((blocks, height, LANES), jnp.float32),
        compiler_params=pltpu.CompilerParams(vmem_limit_bytes=SOME_VMEM),
    )(corrected, right)


def halve_kernel(got_ref, sent_ref):
    count, high = sent_ref.shape[0], got_ref.shape[1]
    half = LANES // 2
    tiles = count // 2
    small = sent_ref.shape[1] // 3
    rows = (high - small) // tiles

    def total(start, size):
        found = got_ref[0, start : start + size, :]
        for peer in range(1, got_ref.shape[0]):
            found += got_ref[peer, start : start + size, :]
        return found

    left = total(tiles * rows, small)
    low = lax.broadcasted_iota(jnp.int32, (rows // 2, LANES), 1) < half
    for tile in range(tiles):
        upper, lower = total(tile * rows, rows // 2), total(tile * rows + rows // 2, rows // 2)
        sent_ref[2 * tile, : rows // 2, :] = jnp.where(low, upper, pltpu.roll(lower, half, 1))
        sent_ref[2 * tile + 1, : rows // 2, :] = jnp.where(low, pltpu.roll(upper, half, 1), lower)
        sent_ref[2 * tile, rows // 2 :, :] = left
        sent_ref[2 * tile + 1, rows // 2 :, :] = left


def halve(got, rows, small, pairs):
    near = pl.BlockSpec(memory_space=pltpu.VMEM)
    return pl.pallas_call(
        halve_kernel,
        in_specs=[near],
        out_specs=near,
        out_shape=jax.ShapeDtypeStruct((pairs, rows // 2 + small, LANES), jnp.float32),
        compiler_params=pltpu.CompilerParams(vmem_limit_bytes=SOME_VMEM),
    )(got)


def middle_kernel(got_ref, sent_ref, left_ref):
    rows, rank = left_ref.shape
    half, groups = LANES // 2, LANES // rank
    found = got_ref[0]
    for peer in range(1, got_ref.shape[0]):
        found += got_ref[peer]
    own, dense = found[: rows // 2, :], found[rows // 2 :, :]
    left = jnp.concatenate([dense[:, g * rank : (g + 1) * rank] for g in range(groups)], axis=0)
    left_ref[...] = left
    turned = left.T
    upper = jnp.dot(turned[:, : rows // 2], own, precision=HIGHEST, preferred_element_type=jnp.float32)
    lower = jnp.dot(turned[:, rows // 2 :], own, precision=HIGHEST, preferred_element_type=jnp.float32)
    first = upper + pltpu.roll(lower, half, 1)
    second = pltpu.roll(upper, half, 1) + lower
    low = lax.broadcasted_iota(jnp.int32, (rank // 2, LANES), 1) < half
    part = jnp.where(low, first[: rank // 2, :], second[rank // 2 :, :])
    gram = jnp.dot(turned, left, precision=HIGHEST, preferred_element_type=jnp.float32)
    high = rank // groups
    gram = jnp.concatenate([gram[g * high : (g + 1) * high, :] for g in range(groups)], axis=1)
    for peer in range(sent_ref.shape[0]):
        sent_ref[peer, : rank // 2, :] = part
        sent_ref[peer, rank // 2 :, :] = gram


def middle(got, rows, rank, peers):
    near = pl.BlockSpec(memory_space=pltpu.VMEM)
    return pl.pallas_call(
        middle_kernel,
        in_specs=[near],
        out_specs=[near, near],
        out_shape=[
            jax.ShapeDtypeStruct((peers, rank // 2 + rank * rank // LANES, LANES), jnp.float32),
            jax.ShapeDtypeStruct((rows, rank), jnp.float32),
        ],
        compiler_params=pltpu.CompilerParams(vmem_limit_bytes=SOME_VMEM),
    )(got)


def solve_kernel(gram_ref, left_ref, back_ref, *, replicas):
    rank = left_ref.shape[1]
    small = gram_ref[0]
    for peer in range(1, gram_ref.shape[0]):
        small += gram_ref[peer]
    gram = jnp.concatenate([small[:, g * rank : (g + 1) * rank] for g in range(LANES // rank)], axis=0)
    row_of = lax.broadcasted_iota(jnp.int32, (rank, rank), 0)
    unit = row_of == lax.broadcasted_iota(jnp.int32, (rank, rank), 1)
    both = jnp.concatenate([gram, unit.astype(jnp.float32)], axis=1)
    below = lax.broadcasted_iota(jnp.int32, (rank, 1), 0)
    for k in range(rank):
        factor = jnp.where(below > k, both[:, k : k + 1], 0.0) / both[k : k + 1, k : k + 1]
        both = both - factor * both[k : k + 1, :]
    pivots = jnp.sum(jnp.where(unit, both[:, :rank], 0.0), axis=0, keepdims=True)
    inverse = both[:, rank:]
    basis = lax.dot_general(
        left_ref[...], inverse, (((1,), (1,)), ((), ())), precision=HIGHEST, preferred_element_type=jnp.float32
    )
    basis = basis / (pivots * replicas)
    back_ref[...] = jnp.dot(basis, inverse, precision=HIGHEST, preferred_element_type=jnp.float32)


def solve(gram, left_sum, replicas):
    peers, height, lanes = gram.shape
    rows, rank = left_sum.shape
    high = rank * rank // LANES
    return pl.pallas_call(
        functools.partial(solve_kernel, replicas=float(replicas)),
        grid=(1,),
        in_specs=[
            pl.BlockSpec((peers, high, lanes), lambda i: (0, height // high - 1, 0)),
            pl.BlockSpec((rows, rank), lambda i: (0, 0)),
        ],
        out_specs=pl.BlockSpec((rows, rank), lambda i: (0, 0)),
        out_shape=jax.ShapeDtypeStruct((rows, rank), jnp.float32),
        compiler_params=pltpu.CompilerParams(vmem_limit_bytes=SOME_VMEM),
        cost_estimate=pl.CostEstimate(flops=4 * rank**3, bytes_accessed=2 * rows * LANES * 4, transcendentals=rank * rank),
    )(gram, left_sum)


def last_kernel(back_ref, whole_ref, sent_ref, averaged_ref, error_ref, averaged, error, leave):
    rows = back_ref.shape[0]
    count, pairs = whole_ref.shape[0], whole_ref.shape[1] // 2
    span = pairs * LANES
    low = lax.broadcasted_iota(jnp.int32, whole_ref.shape[2:], 1) < LANES // 2
    going = []
    for block in range(count):
        upper, lower = [], []
        for pair in range(pairs):
            even, odd = whole_ref[block, 2 * pair], whole_ref[block, 2 * pair + 1]
            upper.append(jnp.where(low, even, pltpu.roll(odd, LANES // 2, 1)))
            lower.append(jnp.where(low, pltpu.roll(even, LANES // 2, 1), odd))
        right = jnp.concatenate([jnp.concatenate(upper, axis=1), jnp.concatenate(lower, axis=1)], axis=0)
        columns = pl.ds(block * span, span)
        found = jnp.dot(back_ref[...], right, precision=HIGHEST, preferred_element_type=jnp.float32)
        averaged[block] = found
        for tile in range(pairs):
            lanes = slice(tile * LANES, (tile + 1) * LANES)
            error[block, :, lanes] = sent_ref[block, tile * rows : (tile + 1) * rows, :] - found[:, lanes]
        going.append(pltpu.make_async_copy(averaged.at[block], averaged_ref.at[:, columns], leave.at[0, block]))
        going.append(pltpu.make_async_copy(error.at[block], error_ref.at[0, :, columns], leave.at[1, block]))
        going[-2].start()
        going[-1].start()
    for copy in going:
        copy.wait()


def last(back, whole, sent):
    rows = back.shape[0]
    blocks = sent.shape[0]
    span = whole.shape[1] * LANES // 2
    near, anywhere = pl.BlockSpec(memory_space=pltpu.VMEM), pl.BlockSpec(memory_space=pl.ANY)
    return pl.pallas_call(
        last_kernel,
        in_specs=[near, near, near],
        out_specs=[anywhere, anywhere],
        out_shape=[
            jax.ShapeDtypeStruct((rows, blocks * span), jnp.float32),
            jax.ShapeDtypeStruct((1, rows, blocks * span), jnp.float32),
        ],
        scratch_shapes=[
            pltpu.VMEM((blocks, rows, span), jnp.float32),
            pltpu.VMEM((blocks, rows, span), jnp.float32),
            pltpu.SemaphoreType.DMA((2, blocks)),
        ],
        compiler_params=pltpu.CompilerParams(vmem_limit_bytes=SOME_VMEM),
    )(back, whole, sent)


def shards(gradient, error_buffer, right_factor):
    rank = right_factor.shape[1]
    rows = gradient.shape[1]
    close, far = lax.axis_size(CLOSE), lax.axis_size("far")

    corrected = gradient[0] + error_buffer[0]
    sent = first(corrected, right_factor.T, close)
    got = lax.all_to_all(sent, CLOSE, 0, 0)
    got = lax.all_to_all(halve(got, rows, rows * rank // LANES, far), "far", 0, 0)

    got, left_sum = middle(got, rows, rank, lax.axis_size(TENSOR))
    got = lax.all_to_all(got, TENSOR, 0, 0)
    back = solve(got, left_sum, lax.axis_size(DP))
    whole = copies(copies(got[:, : rank // 2].sum(0), "far"), CLOSE)
    averaged, new_error = last(back, whole, sent)
    return (averaged, new_error)


def solution(mesh):
    fine = Mesh(mesh.devices.reshape(8, 2, 4, 4, 2), AXES)
    in_specs = (P(DP, TENSOR, None), P(DP, TENSOR, None), P())
    out_specs = (P(TENSOR, None), P(DP, TENSOR, None))
    return jax.shard_map(shards, mesh=fine, in_specs=in_specs, out_specs=out_specs, check_vma=False)
```

```python
import functools

import jax
import jax.numpy as jnp
from jax import lax
from jax.experimental import pallas as pl
from jax.experimental.pallas import tpu as pltpu
from jax.sharding import Mesh, PartitionSpec as P

AXES = ("far", "near", "x", "y", "core")
DP = ("far", "near", "x")
TENSOR = ("y", "core")
CLOSE = ("near", "x")
HIGHEST = lax.Precision.HIGHEST
LANES = 128
SOME_VMEM = 16 * 2**20


def copies(block, axis):
    count = lax.axis_size(axis)
    return lax.all_to_all(jnp.broadcast_to(block[None], (count,) + block.shape), axis, 0, 0)


def first_kernel(corrected_ref, right_ref, sent_ref):
    rows, width = corrected_ref.shape
    rank, count = right_ref.shape[0], sent_ref.shape[0]
    span = width // count
    tiles = span // LANES
    total = None
    for block in range(count):
        columns = slice(block * span, (block + 1) * span)
        corrected = corrected_ref[:, columns]
        for tile in range(tiles):
            sent_ref[block, tile * rows : (tile + 1) * rows, :] = corrected[:, tile * LANES : (tile + 1) * LANES]
        part = lax.dot_general(
            corrected, right_ref[:, columns], (((1,), (1,)), ((), ())), precision=HIGHEST, preferred_element_type=jnp.float32
        )
        total = part if total is None else total + part
    groups = LANES // rank
    high = rows // groups
    dense = jnp.concatenate([total[g * high : (g + 1) * high, :] for g in range(groups)], axis=1)
    for block in range(count):
        sent_ref[block, tiles * rows :, :] = dense


def first(corrected, right, blocks):
    rank, width = right.shape
    rows = corrected.shape[0]
    height = rows * (width // blocks) // LANES + rows * rank // LANES
    near = pl.BlockSpec(memory_space=pltpu.VMEM)
    return pl.pallas_call(
        first_kernel,
        in_specs=[near, near],
        out_specs=near,
        out_shape=jax.ShapeDtypeStruct((blocks, height, LANES), jnp.float32),
        compiler_params=pltpu.CompilerParams(vmem_limit_bytes=SOME_VMEM),
    )(corrected, right)


def halve_kernel(got_ref, sent_ref):
    count, high = sent_ref.shape[0], got_ref.shape[1]
    half = LANES // 2
    tiles = count // 2
    small = sent_ref.shape[1] // 3
    rows = (high - small) // tiles

    def total(start, size):
        found = got_ref[0, start : start + size, :]
        for peer in range(1, got_ref.shape[0]):
            found += got_ref[peer, start : start + size, :]
        return found

    left = total(tiles * rows, small)
    low = lax.broadcasted_iota(jnp.int32, (rows // 2, LANES), 1) < half
    for tile in range(tiles):
        upper, lower = total(tile * rows, rows // 2), total(tile * rows + rows // 2, rows // 2)
        sent_ref[2 * tile, : rows // 2, :] = jnp.where(low, upper, pltpu.roll(lower, half, 1))
        sent_ref[2 * tile + 1, : rows // 2, :] = jnp.where(low, pltpu.roll(upper, half, 1), lower)
        sent_ref[2 * tile, rows // 2 :, :] = left
        sent_ref[2 * tile + 1, rows // 2 :, :] = left


def halve(got, rows, small, pairs):
    near = pl.BlockSpec(memory_space=pltpu.VMEM)
    return pl.pallas_call(
        halve_kernel,
        in_specs=[near],
        out_specs=near,
        out_shape=jax.ShapeDtypeStruct((pairs, rows // 2 + small, LANES), jnp.float32),
        compiler_params=pltpu.CompilerParams(vmem_limit_bytes=SOME_VMEM),
    )(got)


def middle_kernel(got_ref, sent_ref, left_ref):
    rows, rank = left_ref.shape
    half, groups = LANES // 2, LANES // rank
    found = got_ref[0]
    for peer in range(1, got_ref.shape[0]):
        found += got_ref[peer]
    own, dense = found[: rows // 2, :], found[rows // 2 :, :]
    left = jnp.concatenate([dense[:, g * rank : (g + 1) * rank] for g in range(groups)], axis=0)
    left_ref[...] = left
    turned = left.T
    upper = jnp.dot(turned[:, : rows // 2], own, precision=HIGHEST, preferred_element_type=jnp.float32)
    lower = jnp.dot(turned[:, rows // 2 :], own, precision=HIGHEST, preferred_element_type=jnp.float32)
    first = upper + pltpu.roll(lower, half, 1)
    second = pltpu.roll(upper, half, 1) + lower
    low = lax.broadcasted_iota(jnp.int32, (rank // 2, LANES), 1) < half
    part = jnp.where(low, first[: rank // 2, :], second[rank // 2 :, :])
    gram = jnp.dot(turned, left, precision=HIGHEST, preferred_element_type=jnp.float32)
    high = rank // groups
    gram = jnp.concatenate([gram[g * high : (g + 1) * high, :] for g in range(groups)], axis=1)
    share = rank // 4
    for peer in range(sent_ref.shape[0]):
        core = peer % 2
        sent_ref[peer, :share, :] = part[core * share : (core + 1) * share, :]
        sent_ref[peer, share:, :] = gram


def middle(got, rows, rank, peers):
    near = pl.BlockSpec(memory_space=pltpu.VMEM)
    return pl.pallas_call(
        middle_kernel,
        in_specs=[near],
        out_specs=[near, near],
        out_shape=[
            jax.ShapeDtypeStruct((peers, rank // 4 + rank * rank // LANES, LANES), jnp.float32),
            jax.ShapeDtypeStruct((rows, rank), jnp.float32),
        ],
        compiler_params=pltpu.CompilerParams(vmem_limit_bytes=SOME_VMEM),
    )(got)


def solve_kernel(gram_ref, left_ref, back_ref, *, replicas):
    rank = left_ref.shape[1]
    small = gram_ref[0]
    for peer in range(1, gram_ref.shape[0]):
        small += gram_ref[peer]
    gram = jnp.concatenate([small[:, g * rank : (g + 1) * rank] for g in range(LANES // rank)], axis=0)
    row_of = lax.broadcasted_iota(jnp.int32, (rank, rank), 0)
    unit = row_of == lax.broadcasted_iota(jnp.int32, (rank, rank), 1)
    both = jnp.concatenate([gram, unit.astype(jnp.float32)], axis=1)
    below = lax.broadcasted_iota(jnp.int32, (rank, 1), 0)
    for k in range(rank):
        factor = jnp.where(below > k, both[:, k : k + 1], 0.0) / both[k : k + 1, k : k + 1]
        both = both - factor * both[k : k + 1, :]
    pivots = jnp.sum(jnp.where(unit, both[:, :rank], 0.0), axis=0, keepdims=True)
    inverse = both[:, rank:]
    basis = lax.dot_general(
        left_ref[...], inverse, (((1,), (1,)), ((), ())), precision=HIGHEST, preferred_element_type=jnp.float32
    )
    basis = basis / (pivots * replicas)
    back_ref[...] = jnp.dot(basis, inverse, precision=HIGHEST, preferred_element_type=jnp.float32)


def solve(gram, left_sum, replicas):
    peers, height, lanes = gram.shape
    rows, rank = left_sum.shape
    high = rank * rank // LANES
    return pl.pallas_call(
        functools.partial(solve_kernel, replicas=float(replicas)),
        grid=(1,),
        in_specs=[
            pl.BlockSpec((peers, high, lanes), lambda i: (0, height // high - 1, 0)),
            pl.BlockSpec((rows, rank), lambda i: (0, 0)),
        ],
        out_specs=pl.BlockSpec((rows, rank), lambda i: (0, 0)),
        out_shape=jax.ShapeDtypeStruct((rows, rank), jnp.float32),
        compiler_params=pltpu.CompilerParams(vmem_limit_bytes=SOME_VMEM),
        cost_estimate=pl.CostEstimate(flops=4 * rank**3, bytes_accessed=2 * rows * LANES * 4, transcendentals=rank * rank),
    )(gram, left_sum)


def last_kernel(back_ref, whole_ref, sent_ref, averaged_ref, error_ref, averaged, error, leave):
    rows = back_ref.shape[0]
    count, pairs = whole_ref.shape[1], whole_ref.shape[2] // 2
    span = pairs * LANES
    low = lax.broadcasted_iota(jnp.int32, (2 * whole_ref.shape[3], LANES), 1) < LANES // 2

    def of_both(block, at):
        return jnp.concatenate([whole_ref[0, block, at], whole_ref[1, block, at]], axis=0)

    going = []
    for block in range(count):
        upper, lower = [], []
        for pair in range(pairs):
            even, odd = of_both(block, 2 * pair), of_both(block, 2 * pair + 1)
            upper.append(jnp.where(low, even, pltpu.roll(odd, LANES // 2, 1)))
            lower.append(jnp.where(low, pltpu.roll(even, LANES // 2, 1), odd))
        right = jnp.concatenate([jnp.concatenate(upper, axis=1), jnp.concatenate(lower, axis=1)], axis=0)
        columns = pl.ds(block * span, span)
        found = jnp.dot(back_ref[...], right, precision=HIGHEST, preferred_element_type=jnp.float32)
        averaged[block] = found
        for tile in range(pairs):
            lanes = slice(tile * LANES, (tile + 1) * LANES)
            error[block, :, lanes] = sent_ref[block, tile * rows : (tile + 1) * rows, :] - found[:, lanes]
        going.append(pltpu.make_async_copy(averaged.at[block], averaged_ref.at[:, columns], leave.at[0, block]))
        going.append(pltpu.make_async_copy(error.at[block], error_ref.at[0, :, columns], leave.at[1, block]))
        going[-2].start()
        going[-1].start()
    for copy in going:
        copy.wait()


def last(back, whole, sent):
    rows = back.shape[0]
    blocks = sent.shape[0]
    span = whole.shape[2] * LANES // 2
    near, anywhere = pl.BlockSpec(memory_space=pltpu.VMEM), pl.BlockSpec(memory_space=pl.ANY)
    return pl.pallas_call(
        last_kernel,
        in_specs=[near, near, near],
        out_specs=[anywhere, anywhere],
        out_shape=[
            jax.ShapeDtypeStruct((rows, blocks * span), jnp.float32),
            jax.ShapeDtypeStruct((1, rows, blocks * span), jnp.float32),
        ],
        scratch_shapes=[
            pltpu.VMEM((blocks, rows, span), jnp.float32),
            pltpu.VMEM((blocks, rows, span), jnp.float32),
            pltpu.SemaphoreType.DMA((2, blocks)),
        ],
        compiler_params=pltpu.CompilerParams(vmem_limit_bytes=SOME_VMEM),
    )(back, whole, sent)


def shards(gradient, error_buffer, right_factor):
    rank = right_factor.shape[1]
    rows = gradient.shape[1]
    close, far = lax.axis_size(CLOSE), lax.axis_size("far")

    corrected = gradient[0] + error_buffer[0]
    sent = first(corrected, right_factor.T, close)
    got = lax.all_to_all(sent, CLOSE, 0, 0)
    got = lax.all_to_all(halve(got, rows, rows * rank // LANES, far), "far", 0, 0)

    got, left_sum = middle(got, rows, rank, lax.axis_size(TENSOR))
    got = lax.all_to_all(got, TENSOR, 0, 0)
    back = solve(got, left_sum, lax.axis_size(DP))
    whole = lax.all_gather(copies(copies(got[:, : rank // 4].sum(0), "far"), CLOSE), "core")
    averaged, new_error = last(back, whole, sent)
    return (averaged, new_error)


def solution(mesh):
    fine = Mesh(mesh.devices.reshape(8, 2, 4, 4, 2), AXES)
    in_specs = (P(DP, TENSOR, None), P(DP, TENSOR, None), P())
    out_specs = (P(TENSOR, None), P(DP, TENSOR, None))
    return jax.shard_map(shards, mesh=fine, in_specs=in_specs, out_specs=out_specs, check_vma=False)
```

```python
import functools

import jax
import jax.numpy as jnp
from jax import lax
from jax.experimental import pallas as pl
from jax.experimental.pallas import tpu as pltpu
from jax.sharding import Mesh, PartitionSpec as P

AXES = ("far", "near", "x", "y", "core")
DP = ("far", "near", "x")
TENSOR = ("y", "core")
CLOSE = ("near", "x")
HIGHEST = lax.Precision.HIGHEST
LANES = 128
SOME_VMEM = 16 * 2**20


def copies(block, axis):
    count = lax.axis_size(axis)
    return lax.all_to_all(jnp.broadcast_to(block[None], (count,) + block.shape), axis, 0, 0)


def first_kernel(corrected_ref, right_ref, sent_ref):
    rows, width = corrected_ref.shape
    rank, count = right_ref.shape[0], sent_ref.shape[0]
    span = width // count
    tiles = span // LANES
    total = None
    for block in range(count):
        columns = slice(block * span, (block + 1) * span)
        corrected = corrected_ref[:, columns]
        for tile in range(tiles):
            sent_ref[block, tile * rows : (tile + 1) * rows, :] = corrected[:, tile * LANES : (tile + 1) * LANES]
        part = lax.dot_general(
            corrected, right_ref[:, columns], (((1,), (1,)), ((), ())), precision=HIGHEST, preferred_element_type=jnp.float32
        )
        total = part if total is None else total + part
    groups = LANES // rank
    high = rows // groups
    dense = jnp.concatenate([total[g * high : (g + 1) * high, :] for g in range(groups)], axis=1)
    for block in range(count):
        sent_ref[block, tiles * rows :, :] = dense


def first(corrected, right, blocks):
    rank, width = right.shape
    rows = corrected.shape[0]
    height = rows * (width // blocks) // LANES + rows * rank // LANES
    near = pl.BlockSpec(memory_space=pltpu.VMEM)
    return pl.pallas_call(
        first_kernel,
        in_specs=[near, near],
        out_specs=near,
        out_shape=jax.ShapeDtypeStruct((blocks, height, LANES), jnp.float32),
        compiler_params=pltpu.CompilerParams(vmem_limit_bytes=SOME_VMEM),
    )(corrected, right)


def halve_kernel(got_ref, sent_ref):
    count, high = sent_ref.shape[0], got_ref.shape[1]
    half = LANES // 2
    tiles = count // 2
    small = sent_ref.shape[1] // 3
    rows = (high - small) // tiles

    def total(start, size):
        found = got_ref[0, start : start + size, :]
        for peer in range(1, got_ref.shape[0]):
            found += got_ref[peer, start : start + size, :]
        return found

    left = total(tiles * rows, small)
    low = lax.broadcasted_iota(jnp.int32, (rows // 2, LANES), 1) < half
    for tile in range(tiles):
        upper, lower = total(tile * rows, rows // 2), total(tile * rows + rows // 2, rows // 2)
        sent_ref[2 * tile, : rows // 2, :] = jnp.where(low, upper, pltpu.roll(lower, half, 1))
        sent_ref[2 * tile + 1, : rows // 2, :] = jnp.where(low, pltpu.roll(upper, half, 1), lower)
        sent_ref[2 * tile, rows // 2 :, :] = left
        sent_ref[2 * tile + 1, rows // 2 :, :] = left


def halve(got, rows, small, pairs):
    near = pl.BlockSpec(memory_space=pltpu.VMEM)
    return pl.pallas_call(
        halve_kernel,
        in_specs=[near],
        out_specs=near,
        out_shape=jax.ShapeDtypeStruct((pairs, rows // 2 + small, LANES), jnp.float32),
        compiler_params=pltpu.CompilerParams(vmem_limit_bytes=SOME_VMEM),
    )(got)


def middle_kernel(got_ref, sent_ref, left_ref):
    rows, rank = left_ref.shape
    half, groups = LANES // 2, LANES // rank
    found = got_ref[0]
    for peer in range(1, got_ref.shape[0]):
        found += got_ref[peer]
    own, dense = found[: rows // 2, :], found[rows // 2 :, :]
    left = jnp.concatenate([dense[:, g * rank : (g + 1) * rank] for g in range(groups)], axis=0)
    left_ref[...] = left
    turned = left.T
    upper = jnp.dot(turned[:, : rows // 2], own, precision=HIGHEST, preferred_element_type=jnp.float32)
    lower = jnp.dot(turned[:, rows // 2 :], own, precision=HIGHEST, preferred_element_type=jnp.float32)
    first = upper + pltpu.roll(lower, half, 1)
    second = pltpu.roll(upper, half, 1) + lower
    low = lax.broadcasted_iota(jnp.int32, (rank // 2, LANES), 1) < half
    part = jnp.where(low, first[: rank // 2, :], second[rank // 2 :, :])
    gram = jnp.dot(turned, left, precision=HIGHEST, preferred_element_type=jnp.float32)
    high = rank // groups
    gram = jnp.concatenate([gram[g * high : (g + 1) * high, :] for g in range(groups)], axis=1)
    for peer in range(sent_ref.shape[0]):
        sent_ref[peer, : rank // 2, :] = part
        sent_ref[peer, rank // 2 :, :] = gram


def middle(got, rows, rank, peers):
    near = pl.BlockSpec(memory_space=pltpu.VMEM)
    return pl.pallas_call(
        middle_kernel,
        in_specs=[near],
        out_specs=[near, near],
        out_shape=[
            jax.ShapeDtypeStruct((peers, rank // 2 + rank * rank // LANES, LANES), jnp.float32),
            jax.ShapeDtypeStruct((rows, rank), jnp.float32),
        ],
        compiler_params=pltpu.CompilerParams(vmem_limit_bytes=SOME_VMEM),
    )(got)


def solve_kernel(gram_ref, left_ref, back_ref, *, replicas):
    rank = left_ref.shape[1]
    small = gram_ref[0]
    for peer in range(1, gram_ref.shape[0]):
        small += gram_ref[peer]
    gram = jnp.concatenate([small[:, g * rank : (g + 1) * rank] for g in range(LANES // rank)], axis=0)
    row_of = lax.broadcasted_iota(jnp.int32, (rank, rank), 0)
    unit = row_of == lax.broadcasted_iota(jnp.int32, (rank, rank), 1)
    both = jnp.concatenate([gram, unit.astype(jnp.float32)], axis=1)
    below = lax.broadcasted_iota(jnp.int32, (rank, 1), 0)
    for k in range(rank):
        factor = jnp.where(below > k, both[:, k : k + 1], 0.0) / both[k : k + 1, k : k + 1]
        both = both - factor * both[k : k + 1, :]
    pivots = jnp.sum(jnp.where(unit, both[:, :rank], 0.0), axis=0, keepdims=True)
    inverse = both[:, rank:]
    basis = lax.dot_general(
        left_ref[...], inverse, (((1,), (1,)), ((), ())), precision=HIGHEST, preferred_element_type=jnp.float32
    )
    basis = basis / (pivots * replicas)
    back_ref[...] = jnp.dot(basis, inverse, precision=HIGHEST, preferred_element_type=jnp.float32)


def solve(gram, left_sum, replicas):
    peers, height, lanes = gram.shape
    rows, rank = left_sum.shape
    high = rank * rank // LANES
    return pl.pallas_call(
        functools.partial(solve_kernel, replicas=float(replicas)),
        grid=(1,),
        in_specs=[
            pl.BlockSpec((peers, high, lanes), lambda i: (0, height // high - 1, 0)),
            pl.BlockSpec((rows, rank), lambda i: (0, 0)),
        ],
        out_specs=pl.BlockSpec((rows, rank), lambda i: (0, 0)),
        out_shape=jax.ShapeDtypeStruct((rows, rank), jnp.float32),
        compiler_params=pltpu.CompilerParams(vmem_limit_bytes=SOME_VMEM),
        cost_estimate=pl.CostEstimate(flops=4 * rank**3, bytes_accessed=2 * rows * LANES * 4, transcendentals=rank * rank),
    )(gram, left_sum)


def last_kernel(back_ref, whole_ref, sent_ref, averaged_ref, error_ref, averaged, error, leave):
    rows = back_ref.shape[0]
    count, pairs = whole_ref.shape[0], whole_ref.shape[1] // 2
    span = pairs * LANES
    low = lax.broadcasted_iota(jnp.int32, whole_ref.shape[2:], 1) < LANES // 2
    going = []
    for block in range(count):
        upper, lower = [], []
        for pair in range(pairs):
            even, odd = whole_ref[block, 2 * pair], whole_ref[block, 2 * pair + 1]
            upper.append(jnp.where(low, even, pltpu.roll(odd, LANES // 2, 1)))
            lower.append(jnp.where(low, pltpu.roll(even, LANES // 2, 1), odd))
        right = jnp.concatenate([jnp.concatenate(upper, axis=1), jnp.concatenate(lower, axis=1)], axis=0)
        columns = pl.ds(block * span, span)
        found = jnp.dot(back_ref[...], right, precision=HIGHEST, preferred_element_type=jnp.float32)
        averaged[block] = found
        for tile in range(pairs):
            lanes = slice(tile * LANES, (tile + 1) * LANES)
            error[block, :, lanes] = sent_ref[block, tile * rows : (tile + 1) * rows, :] - found[:, lanes]
        going.append(pltpu.make_async_copy(averaged.at[block], averaged_ref.at[:, columns], leave.at[0, block]))
        going.append(pltpu.make_async_copy(error.at[block], error_ref.at[0, :, columns], leave.at[1, block]))
        going[-2].start()
        going[-1].start()
    for copy in going:
        copy.wait()


def last(back, whole, sent):
    rows = back.shape[0]
    blocks = sent.shape[0]
    span = whole.shape[1] * LANES // 2
    near, anywhere = pl.BlockSpec(memory_space=pltpu.VMEM), pl.BlockSpec(memory_space=pl.ANY)
    return pl.pallas_call(
        last_kernel,
        in_specs=[near, near, near],
        out_specs=[anywhere, anywhere],
        out_shape=[
            jax.ShapeDtypeStruct((rows, blocks * span), jnp.float32),
            jax.ShapeDtypeStruct((1, rows, blocks * span), jnp.float32),
        ],
        scratch_shapes=[
            pltpu.VMEM((blocks, rows, span), jnp.float32),
            pltpu.VMEM((blocks, rows, span), jnp.float32),
            pltpu.SemaphoreType.DMA((2, blocks)),
        ],
        compiler_params=pltpu.CompilerParams(vmem_limit_bytes=SOME_VMEM),
    )(back, whole, sent)


def shards(gradient, error_buffer, right_factor):
    rank = right_factor.shape[1]
    rows = gradient.shape[1]
    close, far = lax.axis_size(CLOSE), lax.axis_size("far")

    corrected = gradient[0] + error_buffer[0]
    sent = first(corrected, right_factor.T, close)
    got = lax.all_to_all(sent, CLOSE, 0, 0)
    got = lax.all_to_all(halve(got, rows, rows * rank // LANES, far), "far", 0, 0)

    got, left_sum = middle(got, rows, rank, lax.axis_size(TENSOR))
    got = lax.all_to_all(got, TENSOR, 0, 0)
    back = solve(got, left_sum, lax.axis_size(DP))
    mine = copies(got[:, : rank // 2].sum(0), "far")
    mine, back = lax.optimization_barrier((mine, back))
    whole = copies(mine, CLOSE)
    averaged, new_error = last(back, whole, sent)
    return (averaged, new_error)


def solution(mesh):
    fine = Mesh(mesh.devices.reshape(8, 2, 4, 4, 2), AXES)
    in_specs = (P(DP, TENSOR, None), P(DP, TENSOR, None), P())
    out_specs = (P(TENSOR, None), P(DP, TENSOR, None))
    return jax.shard_map(shards, mesh=fine, in_specs=in_specs, out_specs=out_specs, check_vma=False)
```
